256 devices in a mesh: rep: 2 (over core), shard: 128 (over y, x, z).
Axes of the slice: x: 4, y: 4, z: 8, core: 2. Of those that a mesh axis runs over, the one named last changes fastest.
Arguments:
- gradients: float32 [2, 88, 1024, 1024], P('rep', None, 'shard'), may hold values from -0.2 to 0.2
- left_stats: float32 [88, 1024, 1024], P(None, 'shard', 'rep'), may hold values from -0.09 to 4
- right_stats: float32 [88, 1024, 1024], P(None, 'shard', 'rep'), may hold values from -0.09 to 4
- left_root: bfloat16 [128, 2, 1024, 1024], P('shard', None, None, 'rep'), may hold values from -0.07 to 8, as said below
- right_root: bfloat16 [128, 2, 1024, 1024], P('shard', None, None, 'rep'), may hold values from -0.07 to 8, as said below
- block_owner: int32 [88], replicated, may hold values from 0 to 127, as said below
Outputs:
- left_new: float32 [88, 1024, 1024], P(None, 'shard', 'rep')
- right_new: float32 [88, 1024, 1024], P(None, 'shard', 'rep')
- update: bfloat16 [88, 1024, 1024], P(None, 'shard', 'rep')
The draws below stay inside these ranges and needn't reach their ends.
Inputs may be any that keep to these rules, and one draw needn't show every extreme that they name: `block_owner`: each owner is named by at most 2 blocks; 32 owners are named by exactly two blocks and 24 by exactly one. `left_root`: entry [o, j] belongs to the block that comes j-th, counting from 0 by block index, among those owned by o; entries that no block takes are never read. `right_root`: laid out as left_root.
All inputs are finite; a program needn't handle non-finite values.
Results may differ from the reference program's by a relative error of at most 0.006.
Values may be sent and summed in bfloat16 or wider, within the bound.
No kernel may reach another device: no remote copies, remote signals or barrier semaphores. Data moves between devices by JAX's collectives and lax.ppermute only.
A program may use at most 128 MiB of HBM per device.

```python
import math
import jax
import jax.numpy as jnp
from jax import lax

B = 1024
MAXB = 2
NBLK = 88
N_REP = 2
N_SHARD = 128


def heavy_diagonal(key, shape, low, high, spread):
    key_spread, key_diagonal = jax.random.split(key)
    order = shape[-1]
    scattered = jax.random.uniform(key_spread, shape, jnp.float32, -spread, spread)
    diagonal = jnp.exp(jax.random.uniform(key_diagonal, shape, jnp.float32, math.log(low), math.log(high)))
    on_diagonal = jnp.arange(order)[:, None] == jnp.arange(order)[None, :]
    return jnp.where(on_diagonal, diagonal, scattered)


def draw_left_stats(key, part):
    key = jax.random.fold_in(key, 1)
    return heavy_diagonal(key, (NBLK, B, B), 0.5, 4.0, 0.09)


def draw_right_stats(key, part):
    key = jax.random.fold_in(key, 2)
    return heavy_diagonal(key, (NBLK, B, B), 0.5, 4.0, 0.09)


def draw_left_root(key, part):
    key = jax.random.fold_in(key, 3)
    return heavy_diagonal(key, (N_SHARD, MAXB, B, B), 2.0, 8.0, 0.07).astype(jnp.bfloat16)


def draw_right_root(key, part):
    key = jax.random.fold_in(key, 4)
    return heavy_diagonal(key, (N_SHARD, MAXB, B, B), 2.0, 8.0, 0.07).astype(jnp.bfloat16)


def draw_block_owner(key, part):
    key = jax.random.fold_in(key, 5)
    key_owner, key_block = jax.random.split(key)
    owner_order = jax.random.permutation(key_owner, N_SHARD).astype(jnp.int32)
    block_order = jax.random.permutation(key_block, NBLK).astype(jnp.int32)
    ranks = jnp.arange(NBLK, dtype=jnp.int32)
    chosen = jnp.where(ranks < N_SHARD // 2, ranks // 2, ranks - N_SHARD // 4)
    return jnp.zeros((NBLK,), jnp.int32).at[block_order].set(owner_order[chosen])


def shard_levels(rng, extent, pieces, least, high):
    def one(axis_at, parts):
        draws = jax.random.uniform(jax.random.fold_in(jax.random.fold_in(rng, 6), axis_at), (parts,), jnp.float32, least / len(pieces), high / len(pieces))
        return jnp.repeat(jnp.exp(draws), extent[axis_at] // parts).reshape((-1,) + (1,) * (len(extent) - axis_at - 1))

    gain = one(*pieces[0])
    for cut in pieces[1:]:
        gain = gain * one(*cut)
    return gain


def gaussian(own_key, extent, width, reach, cuts=(), kind=jnp.bfloat16):
    entries = width * jax.random.normal(own_key, extent, jnp.float32)
    if cuts:
        entries = entries * shard_levels(own_key, extent, cuts, -0.22, 0.18)
    return jnp.clip(entries, -reach, reach).astype(kind)


def setup_inputs(seed: int = 0) -> dict:
    splits = jax.random.split(jax.random.key(seed), 7)
    return {
        "gradients": gaussian(splits[0], (N_REP, NBLK, B, B), 0.03, 0.2, ((0, 2), (2, 128)), jnp.float32),
        "left_stats": draw_left_stats(jax.random.fold_in(splits[6], 71), 0),
        "right_stats": draw_right_stats(jax.random.fold_in(splits[6], 71), 0),
        "left_root": draw_left_root(jax.random.fold_in(splits[6], 71), 0),
        "right_root": draw_right_root(jax.random.fold_in(splits[6], 71), 0),
        "block_owner": draw_block_owner(jax.random.fold_in(splits[6], 71), 0),
    }


def slot_numbers(block_owner, owners):
    owner_match = (block_owner[:, None] == jnp.arange(owners, dtype=jnp.int32)[None, :]).astype(jnp.int32)
    earlier = jnp.cumsum(owner_match, axis=0) - owner_match
    return jnp.sum(earlier * owner_match, axis=1).astype(jnp.int32)


def reference(gradients, left_stats, right_stats, left_root, right_root, block_owner):
    slot_of = slot_numbers(block_owner, N_SHARD)
    summed = gradients[0] + gradients[1]
    grad_matrix = summed.astype(jnp.bfloat16)

    def one_block(inputs):
        grad_block, left_old, right_old, owner, slot_index = inputs
        left_factor = left_root[owner, slot_index]
        right_factor = right_root[owner, slot_index]
        left_gram = jnp.dot(grad_block, grad_block.T, preferred_element_type=jnp.float32)
        right_gram = jnp.dot(grad_block.T, grad_block, preferred_element_type=jnp.float32)
        applied = jnp.dot(grad_block, right_factor, preferred_element_type=jnp.float32).astype(jnp.bfloat16)
        block_update = jnp.dot(left_factor, applied, preferred_element_type=jnp.float32).astype(jnp.bfloat16)
        return left_old + left_gram, right_old + right_gram, block_update

    left_new, right_new, update = lax.map(one_block, (grad_matrix, left_stats, right_stats, block_owner, slot_of))
    return (left_new, right_new, update)
```

```python
from functools import partial

import jax
import jax.numpy as jnp
from jax import lax
from jax.experimental import pallas as pl
from jax.experimental.pallas import tpu as pltpu
from jax.sharding import PartitionSpec as P

DOUBLE = 32
SINGLE = 24
PIECES = 4
SMEM = pl.BlockSpec(memory_space=pltpu.SMEM)
ANY = pl.BlockSpec(memory_space=pl.ANY)
VMEM_BYTES = 56 * 1024 * 1024


def whole_gram_counts(blocks, owners):
    idle = owners - DOUBLE - SINGLE
    shared = SINGLE // 2
    return idle, idle + shared


def plan_kernel(owner_ref, send_ref, spot_ref, held_ref, rank_ref, idle_ref, single_ref):
    blocks = owner_ref.shape[0]
    owners = held_ref.shape[0]
    idle_blocks, split_from = whole_gram_counts(blocks, owners)
    pieces = 2 * PIECES * (blocks - split_from)

    def clear(o, carry):
        held_ref[o] = 0
        return carry

    lax.fori_loop(0, owners, clear, 0, unroll=8)

    def place(b, carry):
        o = owner_ref[b]
        slot = held_ref[o]
        send_ref[2 * o + slot] = b
        spot_ref[b] = 2 * o + slot
        held_ref[o] = slot + 1
        return carry

    lax.fori_loop(0, blocks, place, 0, unroll=4)

    def fill(o, carry):
        idles, singles = carry
        held = held_ref[o]
        is_idle = held == 0
        is_single = held == 1
        idle_ref[jnp.where(is_idle, idles, owners - 1)] = o
        single_ref[jnp.where(is_single, singles, owners - 1)] = o
        rank_ref[o] = jnp.where(is_idle, idles, singles)
        extra = jnp.where(idles < pieces, split_from + idles // (2 * PIECES), 0)
        send_ref[2 * o] = jnp.where(is_idle, idles, send_ref[2 * o])
        send_ref[2 * o + 1] = jnp.where(
            is_idle,
            extra,
            jnp.where(is_single, idle_blocks + singles // 2, send_ref[2 * o + 1]),
        )
        return (idles + is_idle.astype(jnp.int32), singles + is_single.astype(jnp.int32))

    lax.fori_loop(0, owners, fill, (jnp.int32(0), jnp.int32(0)), unroll=4)


def make_plan(block_owner, owners):
    blocks = block_owner.shape[0]
    sizes = (2 * owners, blocks, owners, owners, owners, owners)
    return pl.pallas_call(
        plan_kernel,
        out_shape=[jax.ShapeDtypeStruct((n,), jnp.int32) for n in sizes],
        in_specs=[SMEM],
        out_specs=[SMEM] * len(sizes),
        cost_estimate=pl.CostEstimate(flops=0, bytes_accessed=8192, transcendentals=0),
        name="plan",
    )(block_owner)


def dispatch_kernel(side_ref, send_ref, mine_ref, other_ref, out_ref):
    step = pl.program_id(0)
    dests = out_ref.shape[0]
    half = mine_ref.shape[-1]

    def one(i, carry):
        for slot in range(2):
            b = send_ref[2 * (step * dests + i) + slot]
            out_ref[i, :, slot * half : (slot + 1) * half] = (mine_ref[b] + other_ref[b]).astype(
                jnp.bfloat16
            )
        return carry

    lax.fori_loop(0, dests, one, 0, unroll=4)


def dispatch(side, send, gradient, other, owners):
    blocks, rows, width = gradient.shape
    half = width // 2
    steps = 4
    return pl.pallas_call(
        dispatch_kernel,
        grid_spec=pltpu.PrefetchScalarGridSpec(
            num_scalar_prefetch=2,
            grid=(steps,),
            in_specs=[
                pl.BlockSpec((blocks, rows, half), lambda i, side, send: (0, 0, side[0])),
                pl.BlockSpec((blocks, rows, half), lambda i, side, send: (0, 0, 0)),
            ],
            out_specs=pl.BlockSpec(
                (owners // steps, rows, width), lambda i, side, send: (i, 0, 0)
            ),
        ),
        out_shape=jax.ShapeDtypeStruct((owners, rows, width), jnp.bfloat16),
        compiler_params=pltpu.CompilerParams(vmem_limit_bytes=VMEM_BYTES),
        cost_estimate=pl.CostEstimate(flops=0, bytes_accessed=5 << 20, transcendentals=0),
        name="dispatch",
    )(side, send, gradient, other)


def jobs_kernel(
    me_ref,
    held_ref,
    rank_ref,
    own_ref,
    other_ref,
    left_own_ref,
    left_other_ref,
    right_ref,
    out_ref,
    grad,
    left,
    right,
    applied,
    sems,
):
    size = own_ref.shape[0]
    half = size // 2
    quarter = half // PIECES
    side = me_ref[0]
    me = me_ref[1]
    held = held_ref[me]
    rank = rank_ref[me]
    here = pl.multiple_of(side * half, half)
    there = pl.multiple_of(half - side * half, half)
    tile = 256

    def columns(start):
        return pl.ds(start, half)

    loads = []
    for slot in range(2):
        part = pl.ds(slot * half, half)
        loads.append(
            [
                (own_ref.at[:, part], grad.at[slot, :, columns(here)]),
                (other_ref.at[:, part], grad.at[slot, :, columns(there)]),
                (right_ref.at[slot], right.at[slot]),
                (left_own_ref.at[slot], left.at[slot, :, columns(here)]),
                (left_other_ref.at[slot], left.at[slot, :, columns(there)]),
            ]
        )
    copies = [
        [
            pltpu.make_async_copy(source, target, sems.at[slot, i])
            for i, (source, target) in enumerate(loads[slot])
        ]
        for slot in range(2)
    ]
    for slot in range(2):
        for copy in copies[slot]:
            copy.start()

    def tiles(body):
        def step(i, carry):
            body(pl.ds(pl.multiple_of(i * tile, tile), tile))
            return carry

        lax.fori_loop(0, size // tile, step, 0)

    def update(slot):
        target = pl.ds(slot * half, half)

        def first(rows):
            applied[rows, :] = jnp.dot(
                grad[slot, rows, :], right[slot], preferred_element_type=jnp.float32
            ).astype(jnp.bfloat16)

        def second(rows):
            out_ref[rows, target] = jnp.dot(
                left[slot, rows, :], applied[...], preferred_element_type=jnp.float32
            ).astype(jnp.bfloat16)

        tiles(first)
        copies[slot][3].wait()
        copies[slot][4].wait()
        tiles(second)

    def left_gram(slot, start, count, target):
        def body(rows):
            out_ref[rows, target] = lax.dot_general(
                grad[slot, rows, :],
                grad[slot, pl.ds(start, count), :],
                (((1,), (1,)), ((), ())),
                preferred_element_type=jnp.float32,
            ).astype(jnp.bfloat16)

        tiles(body)

    def right_gram(slot, start, count, target):
        def body(rows):
            out_ref[rows, target] = lax.dot_general(
                grad[slot, :, rows],
                grad[slot, :, pl.ds(start, count)],
                (((0,), (0,)), ((), ())),
                preferred_element_type=jnp.float32,
            ).astype(jnp.bfloat16)

        tiles(body)

    def skip_left(slot):
        copies[slot][3].wait()
        copies[slot][4].wait()

    first_part = pl.ds(0, half)
    second_part = pl.ds(half, half)
    last_part = pl.ds(size, quarter)

    for copy in copies[0][:3]:
        copy.wait()

    @pl.when(held > 0)
    def _():
        update(0)

    @pl.when(held == 0)
    def _():
        skip_left(0)
        left_gram(0, here, half, first_part)
        right_gram(0, here, half, second_part)

    for copy in copies[1][:3]:
        copy.wait()

    @pl.when(held == 2)
    def _():
        update(1)

    @pl.when(held < 2)
    def _():
        skip_left(1)

    @pl.when((held == 1) & (rank % 2 == 0))
    def _():
        left_gram(1, here, half, second_part)

    @pl.when((held == 1) & (rank % 2 == 1))
    def _():
        right_gram(1, here, half, second_part)

    piece = rank % (2 * PIECES)
    start = pl.multiple_of(here + (piece % PIECES) * quarter, quarter)

    @pl.when((held == 0) & (piece < PIECES))
    def _():
        left_gram(1, start, quarter, last_part)

    @pl.when((held == 0) & (piece >= PIECES))
    def _():
        right_gram(1, start, quarter, last_part)


def run_jobs(me, held, rank, own, other, left_own, left_other, right_own):
    size = own.shape[0]
    half = size // 2
    width = size + half // PIECES
    bf16 = jnp.bfloat16
    return pl.pallas_call(
        jobs_kernel,
        in_specs=[SMEM] * 3 + [ANY] * 5,
        out_specs=pl.BlockSpec(memory_space=pltpu.VMEM),
        out_shape=jax.ShapeDtypeStruct((size, width), bf16),
        scratch_shapes=[
            pltpu.VMEM((2, size, size), bf16),
            pltpu.VMEM((2, size, size), bf16),
            pltpu.VMEM((2, size, half), bf16),
            pltpu.VMEM((size, half), bf16),
            pltpu.SemaphoreType.DMA((2, 5)),
        ],
        compiler_params=pltpu.CompilerParams(vmem_limit_bytes=VMEM_BYTES),
        cost_estimate=pl.CostEstimate(
            flops=8 * size * size * half, bytes_accessed=12 << 20, transcendentals=0
        ),
        name="jobs",
    )(me, held, rank, own, other, left_own, left_other, right_own)


def finish_kernel(
    spot_ref, idle_ref, single_ref, back_ref, left_ref, right_ref, new_left, new_right, update
):
    step = pl.program_id(0)
    count, _, half = left_ref.shape
    owners = back_ref.shape[0]
    quarter = half // PIECES
    blocks = spot_ref.shape[0]
    idle_blocks, split_from = whole_gram_counts(blocks, owners)
    f32 = jnp.float32

    def part(source, slot):
        return back_ref[source, :, slot * half : (slot + 1) * half]

    def one(i, carry):
        b = step * count + i
        spot = spot_ref[b]
        column = pl.multiple_of((spot % 2) * half, half)
        update[i] = back_ref[spot // 2, :, pl.ds(column, half)]

        @pl.when(b < idle_blocks)
        def _():
            source = idle_ref[b]
            new_left[i] = left_ref[i] + part(source, 0).astype(f32)
            new_right[i] = right_ref[i] + part(source, 1).astype(f32)

        @pl.when((b >= idle_blocks) & (b < split_from))
        def _():
            at = 2 * (b - idle_blocks)
            new_left[i] = left_ref[i] + part(single_ref[at], 1).astype(f32)
            new_right[i] = right_ref[i] + part(single_ref[at + 1], 1).astype(f32)

        @pl.when(b >= split_from)
        def _():
            at = 2 * PIECES * (b - split_from)
            for k in range(PIECES):
                span = pl.ds(k * quarter, quarter)
                last = pl.ds(2 * half, quarter)
                new_left[i, :, span] = left_ref[i, :, span] + back_ref[
                    idle_ref[at + k], :, last
                ].astype(f32)
                new_right[i, :, span] = right_ref[i, :, span] + back_ref[
                    idle_ref[at + PIECES + k], :, last
                ].astype(f32)

        return carry

    lax.fori_loop(0, count, one, 0)


def finish(spot, idle, single, back, left_stats, right_stats):
    blocks, rows, half = left_stats.shape
    steps = 4
    piece = pl.BlockSpec((blocks // steps, rows, half), lambda i, *_: (i, 0, 0))
    whole = pl.BlockSpec(back.shape, lambda i, *_: (0, 0, 0))
    stats = jax.ShapeDtypeStruct(left_stats.shape, jnp.float32)
    return pl.pallas_call(
        finish_kernel,
        grid_spec=pltpu.PrefetchScalarGridSpec(
            num_scalar_prefetch=3,
            grid=(steps,),
            in_specs=[whole, piece, piece],
            out_specs=[piece, piece, piece],
        ),
        out_shape=[stats, stats, jax.ShapeDtypeStruct(left_stats.shape, jnp.bfloat16)],
        compiler_params=pltpu.CompilerParams(vmem_limit_bytes=VMEM_BYTES),
        cost_estimate=pl.CostEstimate(flops=0, bytes_accessed=9 << 20, transcendentals=0),
        name="finish",
    )(spot, idle, single, back, left_stats, right_stats)


def per_device(gradients, left_stats, right_stats, left_root, right_root, block_owner):
    owners = lax.axis_size("shard")
    blocks, rows, half = left_stats.shape
    size = 2 * half
    side = lax.axis_index("rep")
    swapped = partial(lax.ppermute, axis_name="rep", perm=[(0, 1), (1, 0)])
    me = jnp.stack([side, lax.axis_index("shard")]).astype(jnp.int32)
    gradient = gradients[0]
    away = lax.dynamic_slice_in_dim(gradient, half - side * half, half, 2)
    other_gradient = swapped(away)
    send, spot, held, rank, idle, single = make_plan(block_owner, owners)
    outgoing = dispatch(me[:1], send, gradient, other_gradient, owners)
    other_left = swapped(left_root[0])
    arrived = lax.all_to_all(outgoing, "shard", split_axis=0, concat_axis=0, tiled=True)
    own = arrived.reshape(size, size)
    other = swapped(own)
    results = run_jobs(me, held, rank, own, other, left_root[0], other_left, right_root[0])
    back = lax.all_to_all(
        results.reshape(owners, rows, -1), "shard", split_axis=0, concat_axis=0, tiled=True
    )
    return tuple(finish(spot, idle, single, back, left_stats, right_stats))


def solution(mesh):
    return jax.shard_map(
        per_device,
        mesh=mesh,
        in_specs=(
            P("rep", None, "shard", None),
            P(None, "shard", "rep"),
            P(None, "shard", "rep"),
            P("shard", None, None, "rep"),
            P("shard", None, None, "rep"),
            P(),
        ),
        out_specs=(P(None, "shard", "rep"), P(None, "shard", "rep"), P(None, "shard", "rep")),
        check_vma=False,
    )
```

```python
from functools import partial

import jax
import jax.numpy as jnp
from jax import lax
from jax.experimental import pallas as pl
from jax.experimental.pallas import tpu as pltpu
from jax.sharding import PartitionSpec as P

DOUBLE = 32
SINGLE = 24
PIECES = 4
SMEM = pl.BlockSpec(memory_space=pltpu.SMEM)
WHOLE = pl.BlockSpec(memory_space=pltpu.VMEM)
ANY = pl.BlockSpec(memory_space=pl.ANY)
MIB = 1024 * 1024


def in_hbm(value):
    return pltpu.with_memory_space_constraint(value, pltpu.HBM)


def in_vmem(value):
    return pltpu.with_memory_space_constraint(value, pltpu.VMEM)


def whole_gram_counts(blocks, owners):
    idle = owners - DOUBLE - SINGLE
    shared = SINGLE // 2
    return idle, idle + shared


def plan_kernel(
    owner_ref,
    gradient_ref,
    send_ref,
    spot_ref,
    idle_ref,
    single_ref,
    job_ref,
    mine_ref,
    held_ref,
    sem,
):
    blocks = owner_ref.shape[0]
    owners = held_ref.shape[0]
    half = mine_ref.shape[-1]
    side = lax.axis_index("rep")
    me = lax.axis_index("shard")
    here = pl.ds(pl.multiple_of(side * half, half), half)
    copy = pltpu.make_async_copy(gradient_ref.at[:, :, here], mine_ref, sem)
    copy.start()
    idle_blocks, split_from = whole_gram_counts(blocks, owners)
    pieces = 2 * PIECES * (blocks - split_from)

    def clear(o, carry):
        held_ref[o] = 0
        return carry

    lax.fori_loop(0, owners, clear, 0, unroll=8)

    def place(b, carry):
        o = owner_ref[b]
        slot = held_ref[o]
        send_ref[2 * o + slot] = b
        spot_ref[b] = 2 * o + slot
        held_ref[o] = slot + 1
        return carry

    lax.fori_loop(0, blocks, place, 0, unroll=4)

    def fill(o, carry):
        idles, singles, rank = carry
        held = held_ref[o]
        is_idle = held == 0
        is_single = held == 1
        idle_ref[jnp.where(is_idle, idles, owners - 1)] = o
        single_ref[jnp.where(is_single, singles, owners - 1)] = o
        extra = jnp.where(idles < pieces, split_from + idles // (2 * PIECES), 0)
        send_ref[2 * o] = jnp.where(is_idle, idles, send_ref[2 * o])
        send_ref[2 * o + 1] = jnp.where(
            is_idle,
            extra,
            jnp.where(is_single, idle_blocks + singles // 2, send_ref[2 * o + 1]),
        )
        mine = jnp.where(is_idle, idles, singles)
        return (
            idles + is_idle.astype(jnp.int32),
            singles + is_single.astype(jnp.int32),
            jnp.where(o == me, mine, rank),
        )

    zero = jnp.int32(0)
    job_ref[0] = side
    job_ref[1] = held_ref[me]
    job_ref[2] = lax.fori_loop(0, owners, fill, (zero, zero, zero), unroll=4)[2]
    copy.wait()


def make_plan(block_owner, gradient, owners):
    blocks, rows, width = gradient.shape
    sizes = (2 * owners, blocks, owners, owners, 3)
    *tables, mine = pl.pallas_call(
        plan_kernel,
        out_shape=[jax.ShapeDtypeStruct((n,), jnp.int32) for n in sizes]
        + [jax.ShapeDtypeStruct((blocks, rows, width // 2), jnp.float32)],
        in_specs=[SMEM, ANY],
        out_specs=[SMEM] * len(sizes) + [WHOLE],
        scratch_shapes=[pltpu.SMEM((owners,), jnp.int32), pltpu.SemaphoreType.DMA],
        compiler_params=pltpu.CompilerParams(vmem_limit_bytes=4 * MIB),
        cost_estimate=pl.CostEstimate(flops=0, bytes_accessed=4 << 20, transcendentals=0),
        name="plan",
    )(in_hbm(block_owner), in_hbm(gradient))
    return tables + [mine]


def dispatch_kernel(job_ref, send_ref, mine_ref, other_ref, out_ref):
    dests, _, width = out_ref.shape
    half = width // 2
    here = pl.ds(pl.multiple_of(job_ref[0] * half, half), half)

    def one(dest, carry):
        for slot in range(2):
            b = send_ref[2 * dest + slot]
            out_ref[dest, :, slot * half : (slot + 1) * half] = (
                mine_ref[b] + other_ref[b, :, here]
            ).astype(jnp.bfloat16)
        return carry

    lax.fori_loop(0, dests, one, 0, unroll=4)


def dispatch(job, send, mine, other, owners):
    _, rows, width = other.shape
    return pl.pallas_call(
        dispatch_kernel,
        in_specs=[SMEM, SMEM, WHOLE, WHOLE],
        out_specs=WHOLE,
        out_shape=jax.ShapeDtypeStruct((owners, rows, width), jnp.bfloat16),
        compiler_params=pltpu.CompilerParams(vmem_limit_bytes=16 * MIB),
        cost_estimate=pl.CostEstimate(flops=0, bytes_accessed=5 << 20, transcendentals=0),
        name="dispatch",
    )(job, send, in_vmem(mine), other)


def fetch_kernel(*refs):
    count = len(refs) // 2
    sems = refs[-1]
    copies = [pltpu.make_async_copy(refs[i], refs[count + i], sems.at[i]) for i in range(count)]
    for copy in copies:
        copy.start()
    for copy in copies:
        copy.wait()


def fetch(*values):
    size = sum(value.size * value.dtype.itemsize for value in values)
    fetched = pl.pallas_call(
        fetch_kernel,
        in_specs=[ANY] * len(values),
        out_specs=[WHOLE] * len(values),
        out_shape=[jax.ShapeDtypeStruct(value.shape, value.dtype) for value in values],
        scratch_shapes=[pltpu.SemaphoreType.DMA((len(values),))],
        compiler_params=pltpu.CompilerParams(vmem_limit_bytes=16 * MIB),
        cost_estimate=pl.CostEstimate(flops=0, bytes_accessed=2 * size, transcendentals=0),
        name="fetch",
    )(*[in_hbm(value) for value in values])
    return [in_vmem(value) for value in fetched]


def jobs_kernel(
    job_ref, own_ref, other_ref, left_own, left_other, right, out_ref, applied
):
    size, width = own_ref.shape
    half = width // 2
    quarter = half // PIECES
    side = job_ref[0]
    held = job_ref[1]
    rank = job_ref[2]
    here = pl.multiple_of(side * half, half)
    there = pl.multiple_of(half - side * half, half)
    tile = 512

    def tiles(count, body):
        for at in range(0, count, tile):
            body(at)

    def rows_at(start):
        return pl.ds(pl.multiple_of(start, tile), tile)

    def product(a, b, dims):
        return lax.dot_general(
            a, b, ((dims[:1], dims[1:]), ((), ())), preferred_element_type=jnp.float32
        )

    def update(slot):
        span = pl.ds(slot * half, half)

        def first(at):
            rows = rows_at(at)
            total = product(own_ref[rows, span], right[slot, pl.ds(here, half), :], (1, 0))
            total += product(other_ref[rows, span], right[slot, pl.ds(there, half), :], (1, 0))
            applied[rows, :] = total.astype(jnp.bfloat16)

        def second(at):
            rows = rows_at(at)
            total = product(left_own[slot, rows, :], applied[pl.ds(here, half), :], (1, 0))
            total += product(left_other[slot, rows, :], applied[pl.ds(there, half), :], (1, 0))
            out_ref[rows, span] = total.astype(jnp.bfloat16)

        tiles(size, first)
        tiles(size, second)

    def left_gram(slot, start, count, target):
        span = pl.ds(slot * half, half)
        wanted = pl.ds(pl.multiple_of(here + start, quarter), count)

        def body(at):
            rows = rows_at(at)
            total = product(own_ref[rows, span], own_ref[wanted, span], (1, 1))
            total += product(other_ref[rows, span], other_ref[wanted, span], (1, 1))
            out_ref[rows, target] = total.astype(jnp.bfloat16)

        tiles(size, body)

    def right_gram(slot, start, count, target):
        wanted = pl.ds(pl.multiple_of(slot * half + start, quarter), count)
        for source, offset in ((own_ref, here), (other_ref, there)):

            def body(at):
                span = pl.ds(pl.multiple_of(slot * half + at, tile), tile)
                total = product(source[:, span], own_ref[:, wanted], (0, 0))
                out_ref[rows_at(offset + at), target] = total.astype(jnp.bfloat16)

            tiles(half, body)

    first_part = pl.ds(0, half)
    second_part = pl.ds(half, half)
    last_part = pl.ds(width, quarter)

    @pl.when(held > 0)
    def _():
        update(0)

    @pl.when(held == 0)
    def _():
        left_gram(0, 0, half, first_part)
        right_gram(0, 0, half, second_part)

    @pl.when(held == 2)
    def _():
        update(1)

    @pl.when((held == 1) & (rank % 2 == 0))
    def _():
        left_gram(1, 0, half, second_part)

    @pl.when((held == 1) & (rank % 2 == 1))
    def _():
        right_gram(1, 0, half, second_part)

    piece = rank % (2 * PIECES)
    start = (piece % PIECES) * quarter

    @pl.when((held == 0) & (piece < PIECES))
    def _():
        left_gram(1, start, quarter, last_part)

    @pl.when((held == 0) & (piece >= PIECES))
    def _():
        right_gram(1, start, quarter, last_part)


def run_jobs(job, own, other, left_own, left_other, right_own):
    size = own.shape[0]
    half = size // 2
    width = size + half // PIECES
    bf16 = jnp.bfloat16
    return pl.pallas_call(
        jobs_kernel,
        in_specs=[SMEM] + [WHOLE] * 5,
        out_specs=WHOLE,
        out_shape=jax.ShapeDtypeStruct((size, width), bf16),
        scratch_shapes=[pltpu.VMEM((size, half), bf16)],
        compiler_params=pltpu.CompilerParams(vmem_limit_bytes=20 * MIB),
        cost_estimate=pl.CostEstimate(
            flops=8 * size * size * half, bytes_accessed=12 << 20, transcendentals=0
        ),
        name="jobs",
    )(job, own, other, left_own, left_other, right_own)


def finish_kernel(
    spot_ref,
    idle_ref,
    single_ref,
    back_ref,
    left_ref,
    right_ref,
    left_out,
    right_out,
    update_out,
    new_left,
    new_right,
    update,
    sems,
):
    blocks, _, half = left_ref.shape
    owners = back_ref.shape[0]
    quarter = half // PIECES
    idle_blocks, split_from = whole_gram_counts(blocks, owners)
    f32 = jnp.float32

    def part(source, slot):
        return back_ref[source, :, slot * half : (slot + 1) * half].astype(f32)

    def applied(b):
        spot = spot_ref[b]
        column = pl.multiple_of((spot % 2) * half, half)
        update[b] = back_ref[spot // 2, :, pl.ds(column, half)]

    def whole_pair(b, carry):
        applied(b)
        source = idle_ref[b]
        new_left[b] = left_ref[b] + part(source, 0)
        new_right[b] = right_ref[b] + part(source, 1)
        return carry

    def shared_pair(b, carry):
        applied(b)
        at = 2 * (b - idle_blocks)
        new_left[b] = left_ref[b] + part(single_ref[at], 1)
        new_right[b] = right_ref[b] + part(single_ref[at + 1], 1)
        return carry

    def split_pair(b, carry):
        applied(b)
        at = 2 * PIECES * (b - split_from)
        last = pl.ds(2 * half, quarter)
        for k in range(PIECES):
            span = pl.ds(k * quarter, quarter)
            for new, old, source in (
                (new_left, left_ref, idle_ref[at + k]),
                (new_right, right_ref, idle_ref[at + PIECES + k]),
            ):
                new[b, :, span] = old[b, :, span] + back_ref[source, :, last].astype(f32)
        return carry

    copies = []

    def send(first, last):
        span = pl.ds(first, last - first)
        for source, target in ((new_left, left_out), (new_right, right_out), (update, update_out)):
            copy = pltpu.make_async_copy(source.at[span], target.at[span], sems.at[len(copies)])
            copy.start()
            copies.append(copy)

    third = idle_blocks // 3
    for first in range(0, idle_blocks, third):
        lax.fori_loop(first, first + third, whole_pair, 0, unroll=2)
        send(first, first + third)
    lax.fori_loop(idle_blocks, split_from, shared_pair, 0, unroll=2)
    lax.fori_loop(split_from, blocks, split_pair, 0)
    send(idle_blocks, blocks)
    for copy in copies:
        copy.wait()


def finish(spot, idle, single, back, left_stats, right_stats):
    shape = left_stats.shape
    kinds = (jnp.float32, jnp.float32, jnp.bfloat16)
    return pl.pallas_call(
        finish_kernel,
        in_specs=[SMEM] * 3 + [WHOLE] * 3,
        out_specs=[ANY] * 3,
        out_shape=[jax.ShapeDtypeStruct(shape, kind) for kind in kinds],
        scratch_shapes=[pltpu.VMEM(shape, kind) for kind in kinds]
        + [pltpu.SemaphoreType.DMA((12,))],
        compiler_params=pltpu.CompilerParams(vmem_limit_bytes=16 * MIB),
        cost_estimate=pl.CostEstimate(flops=0, bytes_accessed=9 << 20, transcendentals=0),
        name="finish",
    )(spot, idle, single, back, left_stats, right_stats)


def per_device(gradients, left_stats, right_stats, left_root, right_root, block_owner):
    owners = lax.axis_size("shard")
    blocks, rows, half = left_stats.shape
    size = 2 * half
    swapped = partial(lax.ppermute, axis_name="rep", perm=[(0, 1), (1, 0)])
    gradient = gradients[0]
    other_gradient = swapped(gradient)
    send, spot, idle, single, job, mine = make_plan(block_owner, gradient, owners)
    outgoing = dispatch(job, send, mine, other_gradient, owners)
    other_left = swapped(left_root[0])
    arrived = lax.all_to_all(outgoing, "shard", split_axis=0, concat_axis=0, tiled=True)
    own = arrived.reshape(size, size)
    other = swapped(own)
    roots = fetch(left_root[0], other_left, right_root[0])
    results = run_jobs(job, own, other, *roots)
    back = lax.all_to_all(
        results.reshape(owners, rows, -1), "shard", split_axis=0, concat_axis=0, tiled=True
    )
    return tuple(finish(spot, idle, single, back, left_stats, right_stats))


def solution(mesh):
    return jax.shard_map(
        per_device,
        mesh=mesh,
        in_specs=(
            P("rep", None, "shard", None),
            P(None, "shard", "rep"),
            P(None, "shard", "rep"),
            P("shard", None, None, "rep"),
            P("shard", None, None, "rep"),
            P(),
        ),
        out_specs=(P(None, "shard", "rep"), P(None, "shard", "rep"), P(None, "shard", "rep")),
        check_vma=False,
    )
```

```python
from functools import partial

import jax
import jax.numpy as jnp
from jax import lax
from jax.experimental import pallas as pl
from jax.experimental.pallas import tpu as pltpu
from jax.sharding import PartitionSpec as P

DOUBLE = 32
SINGLE = 24
PIECES = 4
SMEM = pl.BlockSpec(memory_space=pltpu.SMEM)
WHOLE = pl.BlockSpec(memory_space=pltpu.VMEM)
ANY = pl.BlockSpec(memory_space=pl.ANY)
MIB = 1024 * 1024
TILE = 512


def in_hbm(value):
    return pltpu.with_memory_space_constraint(value, pltpu.HBM)


def in_vmem(value):
    return pltpu.with_memory_space_constraint(value, pltpu.VMEM)


def whole_gram_counts(blocks, owners):
    idle = owners - DOUBLE - SINGLE
    shared = SINGLE // 2
    return idle, idle + shared


def plan_kernel(
    owner_ref,
    gradient_ref,
    send_ref,
    spot_ref,
    idle_ref,
    single_ref,
    job_ref,
    mine_ref,
    held_ref,
    sem,
):
    blocks = owner_ref.shape[0]
    owners = held_ref.shape[0]
    half = mine_ref.shape[-1]
    side = lax.axis_index("rep")
    me = lax.axis_index("shard")
    here = pl.ds(pl.multiple_of(side * half, half), half)
    copy = pltpu.make_async_copy(gradient_ref.at[:, :, here], mine_ref, sem)
    copy.start()
    idle_blocks, split_from = whole_gram_counts(blocks, owners)
    pieces = 2 * PIECES * (blocks - split_from)

    def clear(o, carry):
        held_ref[o] = 0
        return carry

    lax.fori_loop(0, owners, clear, 0, unroll=8)

    def place(b, carry):
        o = owner_ref[b]
        slot = held_ref[o]
        send_ref[2 * o + slot] = b
        spot_ref[b] = 2 * o + slot
        held_ref[o] = slot + 1
        return carry

    lax.fori_loop(0, blocks, place, 0, unroll=8)

    def fill(o, carry):
        idles, singles, rank = carry
        held = held_ref[o]
        is_idle = held == 0
        is_single = held == 1
        idle_ref[jnp.where(is_idle, idles, owners - 1)] = o
        single_ref[jnp.where(is_single, singles, owners - 1)] = o
        extra = jnp.where(idles < pieces, split_from + idles // (2 * PIECES), 0)
        send_ref[2 * o] = jnp.where(is_idle, idles, send_ref[2 * o])
        send_ref[2 * o + 1] = jnp.where(
            is_idle,
            extra,
            jnp.where(is_single, idle_blocks + singles // 2, send_ref[2 * o + 1]),
        )
        mine = jnp.where(is_idle, idles, singles)
        return (
            idles + is_idle.astype(jnp.int32),
            singles + is_single.astype(jnp.int32),
            jnp.where(o == me, mine, rank),
        )

    zero = jnp.int32(0)
    job_ref[0] = side
    job_ref[1] = held_ref[me]
    job_ref[2] = lax.fori_loop(0, owners, fill, (zero, zero, zero), unroll=8)[2]
    copy.wait()


def make_plan(block_owner, gradient, owners):
    blocks, rows, width = gradient.shape
    sizes = (2 * owners, blocks, owners, owners, 3)
    *tables, mine = pl.pallas_call(
        plan_kernel,
        out_shape=[jax.ShapeDtypeStruct((n,), jnp.int32) for n in sizes]
        + [jax.ShapeDtypeStruct((blocks, rows, width // 2), jnp.float32)],
        in_specs=[SMEM, ANY],
        out_specs=[SMEM] * len(sizes) + [WHOLE],
        scratch_shapes=[pltpu.SMEM((owners,), jnp.int32), pltpu.SemaphoreType.DMA],
        compiler_params=pltpu.CompilerParams(vmem_limit_bytes=4 * MIB),
        cost_estimate=pl.CostEstimate(flops=0, bytes_accessed=4 << 20, transcendentals=0),
        name="plan",
    )(in_hbm(block_owner), in_hbm(gradient))
    return tables + [mine]


def dispatch_kernel(job_ref, send_ref, mine_ref, other_ref, out_ref):
    dests, _, width = out_ref.shape
    half = width // 2
    here = pl.ds(pl.multiple_of(job_ref[0] * half, half), half)

    def one(dest, carry):
        for slot in range(2):
            b = send_ref[2 * dest + slot]
            out_ref[dest, :, slot * half : (slot + 1) * half] = (
                mine_ref[b] + other_ref[b, :, here]
            ).astype(jnp.bfloat16)
        return carry

    lax.fori_loop(0, dests, one, 0, unroll=4)


def dispatch(job, send, mine, other, owners):
    _, rows, width = other.shape
    return pl.pallas_call(
        dispatch_kernel,
        in_specs=[SMEM, SMEM, WHOLE, WHOLE],
        out_specs=WHOLE,
        out_shape=jax.ShapeDtypeStruct((owners, rows, width), jnp.bfloat16),
        compiler_params=pltpu.CompilerParams(vmem_limit_bytes=16 * MIB),
        cost_estimate=pl.CostEstimate(flops=0, bytes_accessed=5 << 20, transcendentals=0),
        name="dispatch",
    )(job, send, in_vmem(mine), other)


def product(a, b, dims):
    return lax.dot_general(
        a, b, ((dims[:1], dims[1:]), ((), ())), preferred_element_type=jnp.float32
    )


def begin_kernel(
    job_ref, own_ref, left_own, left_other, right_own, left_ref, right_ref, total_ref, sems
):
    _, width = own_ref.shape
    half = width // 2
    here = pl.multiple_of(job_ref[0] * half, half)
    there = pl.multiple_of(half - job_ref[0] * half, half)
    held = job_ref[1]
    rights = [
        pltpu.make_async_copy(right_own.at[slot], right_ref.at[slot], sems.at[slot])
        for slot in range(2)
    ]
    lefts = [
        pltpu.make_async_copy(source, left_ref.at[:, :, pl.ds(start, half)], sems.at[2 + i])
        for i, (source, start) in enumerate(((left_own, here), (left_other, there)))
    ]
    for copy in rights + lefts:
        copy.start()
    for slot in range(2):
        rights[slot].wait()

        @pl.when(held > slot)
        def _():
            span = pl.ds(slot * half, half)
            for at in range(0, own_ref.shape[0], TILE):
                rows = pl.ds(at, TILE)
                total_ref[slot, rows, :] = product(
                    own_ref[rows, span], right_ref[slot, pl.ds(here, half), :], (1, 0)
                )

    for copy in lefts:
        copy.wait()


def begin_updates(job, own, left_own, left_other, right_own):
    size = own.shape[0]
    half = size // 2
    bf16 = jnp.bfloat16
    begun = pl.pallas_call(
        begin_kernel,
        in_specs=[SMEM, WHOLE] + [ANY] * 3,
        out_specs=[WHOLE] * 3,
        out_shape=[
            jax.ShapeDtypeStruct((2, size, size), bf16),
            jax.ShapeDtypeStruct((2, size, half), bf16),
            jax.ShapeDtypeStruct((2, size, half), jnp.float32),
        ],
        scratch_shapes=[pltpu.SemaphoreType.DMA((4,))],
        compiler_params=pltpu.CompilerParams(vmem_limit_bytes=20 * MIB),
        cost_estimate=pl.CostEstimate(
            flops=4 * size * half * half, bytes_accessed=16 << 20, transcendentals=0
        ),
        name="begin",
    )(job, own, in_hbm(left_own), in_hbm(left_other), in_hbm(right_own))
    return [in_vmem(value) for value in begun]


def jobs_kernel(
    job_ref, own_ref, other_ref, left, right, total_ref, out_ref, applied
):
    size, width = own_ref.shape
    half = width // 2
    quarter = half // PIECES
    side = job_ref[0]
    held = job_ref[1]
    rank = job_ref[2]
    here = pl.multiple_of(side * half, half)
    there = pl.multiple_of(half - side * half, half)

    def tiles(count, body):
        for at in range(0, count, TILE):
            body(at)

    def rows_at(start):
        return pl.ds(pl.multiple_of(start, TILE), TILE)

    def update(slot):
        span = pl.ds(slot * half, half)

        def first(at):
            rows = rows_at(at)
            total = product(other_ref[rows, span], right[slot, pl.ds(there, half), :], (1, 0))
            total += total_ref[slot, rows, :]
            applied[rows, :] = total.astype(jnp.bfloat16)

        def second(at):
            rows = rows_at(at)
            out_ref[rows, span] = product(left[slot, rows, :], applied[...], (1, 0)).astype(
                jnp.bfloat16
            )

        tiles(size, first)
        tiles(size, second)

    def left_gram(slot, start, count, target):
        span = pl.ds(slot * half, half)
        wanted = pl.ds(pl.multiple_of(here + start, quarter), count)

        def body(at):
            rows = rows_at(at)
            total = product(own_ref[rows, span], own_ref[wanted, span], (1, 1))
            total += product(other_ref[rows, span], other_ref[wanted, span], (1, 1))
            out_ref[rows, target] = total.astype(jnp.bfloat16)

        tiles(size, body)

    def right_gram(slot, start, count, target):
        wanted = pl.ds(pl.multiple_of(slot * half + start, quarter), count)
        for source, offset in ((own_ref, here), (other_ref, there)):

            def body(at):
                span = pl.ds(pl.multiple_of(slot * half + at, TILE), TILE)
                total = product(source[:, span], own_ref[:, wanted], (0, 0))
                out_ref[rows_at(offset + at), target] = total.astype(jnp.bfloat16)

            tiles(half, body)

    first_part = pl.ds(0, half)
    second_part = pl.ds(half, half)
    last_part = pl.ds(width, quarter)

    @pl.when(held > 0)
    def _():
        update(0)

    @pl.when(held == 0)
    def _():
        left_gram(0, 0, half, first_part)
        right_gram(0, 0, half, second_part)

    @pl.when(held == 2)
    def _():
        update(1)

    @pl.when((held == 1) & (rank % 2 == 0))
    def _():
        left_gram(1, 0, half, second_part)

    @pl.when((held == 1) & (rank % 2 == 1))
    def _():
        right_gram(1, 0, half, second_part)

    piece = rank % (2 * PIECES)
    start = (piece % PIECES) * quarter

    @pl.when((held == 0) & (piece < PIECES))
    def _():
        left_gram(1, start, quarter, last_part)

    @pl.when((held == 0) & (piece >= PIECES))
    def _():
        right_gram(1, start, quarter, last_part)


def run_jobs(job, own, other, left, right, total):
    size = own.shape[0]
    half = size // 2
    width = size + half // PIECES
    bf16 = jnp.bfloat16
    return pl.pallas_call(
        jobs_kernel,
        in_specs=[SMEM] + [WHOLE] * 5,
        out_specs=WHOLE,
        out_shape=jax.ShapeDtypeStruct((size, width), bf16),
        scratch_shapes=[pltpu.VMEM((size, half), bf16)],
        compiler_params=pltpu.CompilerParams(vmem_limit_bytes=20 * MIB),
        cost_estimate=pl.CostEstimate(
            flops=8 * size * size * half, bytes_accessed=12 << 20, transcendentals=0
        ),
        name="jobs",
    )(job, own, other, left, right, total)


def finish_kernel(
    spot_ref,
    idle_ref,
    single_ref,
    back_ref,
    left_ref,
    right_ref,
    left_out,
    right_out,
    update_out,
    new_left,
    new_right,
    update,
    sems,
):
    blocks, _, half = left_ref.shape
    owners = back_ref.shape[0]
    quarter = half // PIECES
    idle_blocks, split_from = whole_gram_counts(blocks, owners)
    f32 = jnp.float32

    def part(source, slot):
        return back_ref[source, :, slot * half : (slot + 1) * half].astype(f32)

    def applied(b):
        spot = spot_ref[b]
        column = pl.multiple_of((spot % 2) * half, half)
        update[b] = back_ref[spot // 2, :, pl.ds(column, half)]

    def whole_pair(b, carry):
        applied(b)
        source = idle_ref[b]
        new_left[b] = left_ref[b] + part(source, 0)
        new_right[b] = right_ref[b] + part(source, 1)
        return carry

    def shared_pair(b, carry):
        applied(b)
        at = 2 * (b - idle_blocks)
        new_left[b] = left_ref[b] + part(single_ref[at], 1)
        new_right[b] = right_ref[b] + part(single_ref[at + 1], 1)
        return carry

    def split_pair(b, carry):
        applied(b)
        at = 2 * PIECES * (b - split_from)
        last = pl.ds(2 * half, quarter)
        for k in range(PIECES):
            span = pl.ds(k * quarter, quarter)
            for new, old, source in (
                (new_left, left_ref, idle_ref[at + k]),
                (new_right, right_ref, idle_ref[at + PIECES + k]),
            ):
                new[b, :, span] = old[b, :, span] + back_ref[source, :, last].astype(f32)
        return carry

    copies = []

    def send(first, last):
        span = pl.ds(first, last - first)
        for source, target in ((new_left, left_out), (new_right, right_out), (update, update_out)):
            copy = pltpu.make_async_copy(source.at[span], target.at[span], sems.at[len(copies)])
            copy.start()
            copies.append(copy)

    third = idle_blocks // 3
    for first in range(0, idle_blocks, third):
        lax.fori_loop(first, first + third, whole_pair, 0, unroll=2)
        send(first, first + third)
    lax.fori_loop(idle_blocks, split_from, shared_pair, 0, unroll=2)
    lax.fori_loop(split_from, blocks, split_pair, 0)
    send(idle_blocks, blocks)
    for copy in copies:
        copy.wait()


def finish(spot, idle, single, back, left_stats, right_stats):
    shape = left_stats.shape
    kinds = (jnp.float32, jnp.float32, jnp.bfloat16)
    return pl.pallas_call(
        finish_kernel,
        in_specs=[SMEM] * 3 + [WHOLE] * 3,
        out_specs=[ANY] * 3,
        out_shape=[jax.ShapeDtypeStruct(shape, kind) for kind in kinds],
        scratch_shapes=[pltpu.VMEM(shape, kind) for kind in kinds]
        + [pltpu.SemaphoreType.DMA((12,))],
        compiler_params=pltpu.CompilerParams(vmem_limit_bytes=16 * MIB),
        cost_estimate=pl.CostEstimate(flops=0, bytes_accessed=9 << 20, transcendentals=0),
        name="finish",
    )(spot, idle, single, back, left_stats, right_stats)


def per_device(gradients, left_stats, right_stats, left_root, right_root, block_owner):
    owners = lax.axis_size("shard")
    blocks, rows, half = left_stats.shape
    size = 2 * half
    swapped = partial(lax.ppermute, axis_name="rep", perm=[(0, 1), (1, 0)])
    gradient = gradients[0]
    other_gradient = swapped(gradient)
    send, spot, idle, single, job, mine = make_plan(block_owner, gradient, owners)
    outgoing = dispatch(job, send, mine, other_gradient, owners)
    other_left = swapped(left_root[0])
    arrived = lax.all_to_all(outgoing, "shard", split_axis=0, concat_axis=0, tiled=True)
    own = arrived.reshape(size, size)
    other = swapped(own)
    begun = begin_updates(job, own, left_root[0], other_left, right_root[0])
    results = run_jobs(job, own, other, *begun)
    back = lax.all_to_all(
        results.reshape(owners, rows, -1), "shard", split_axis=0, concat_axis=0, tiled=True
    )
    return tuple(finish(spot, idle, single, back, left_stats, right_stats))


def solution(mesh):
    return jax.shard_map(
        per_device,
        mesh=mesh,
        in_specs=(
            P("rep", None, "shard", None),
            P(None, "shard", "rep"),
            P(None, "shard", "rep"),
            P("shard", None, None, "rep"),
            P("shard", None, None, "rep"),
            P(),
        ),
        out_specs=(P(None, "shard", "rep"), P(None, "shard", "rep"), P(None, "shard", "rep")),
        check_vma=False,
    )
```

```python
from functools import partial

import jax
import jax.numpy as jnp
from jax import lax
from jax.experimental import pallas as pl
from jax.experimental.pallas import tpu as pltpu
from jax.sharding import PartitionSpec as P

DOUBLE = 32
SINGLE = 24
PIECES = 4
SMEM = pl.BlockSpec(memory_space=pltpu.SMEM)
WHOLE = pl.BlockSpec(memory_space=pltpu.VMEM)
ANY = pl.BlockSpec(memory_space=pl.ANY)
MIB = 1024 * 1024
TILE = 512


def in_hbm(value):
    return pltpu.with_memory_space_constraint(value, pltpu.HBM)


def in_vmem(value):
    return pltpu.with_memory_space_constraint(value, pltpu.VMEM)


def whole_gram_counts(blocks, owners):
    idle = owners - DOUBLE - SINGLE
    shared = SINGLE // 2
    return idle, idle + shared


def plan_kernel(
    owner_ref,
    gradient_ref,
    send_ref,
    spot_ref,
    idle_ref,
    single_ref,
    job_ref,
    mine_ref,
    held_ref,
    sem,
):
    blocks = owner_ref.shape[0]
    owners = held_ref.shape[0]
    half = mine_ref.shape[-1]
    side = lax.axis_index("rep")
    me = lax.axis_index("shard")
    here = pl.ds(pl.multiple_of(side * half, half), half)
    copy = pltpu.make_async_copy(gradient_ref.at[:, :, here], mine_ref, sem)
    copy.start()
    idle_blocks, split_from = whole_gram_counts(blocks, owners)
    pieces = 2 * PIECES * (blocks - split_from)

    def clear(o, carry):
        held_ref[o] = 0
        return carry

    lax.fori_loop(0, owners, clear, 0, unroll=8)

    def place(b, carry):
        o = owner_ref[b]
        slot = held_ref[o]
        send_ref[2 * o + slot] = b
        spot_ref[b] = 2 * o + slot
        held_ref[o] = slot + 1
        return carry

    lax.fori_loop(0, blocks, place, 0, unroll=8)

    def fill(o, carry):
        idles, singles, rank = carry
        held = held_ref[o]
        is_idle = held == 0
        is_single = held == 1
        idle_ref[jnp.where(is_idle, idles, owners - 1)] = o
        single_ref[jnp.where(is_single, singles, owners - 1)] = o
        extra = jnp.where(idles < pieces, split_from + idles // (2 * PIECES), 0)
        send_ref[2 * o] = jnp.where(is_idle, idles, send_ref[2 * o])
        send_ref[2 * o + 1] = jnp.where(
            is_idle,
            extra,
            jnp.where(is_single, idle_blocks + singles // 2, send_ref[2 * o + 1]),
        )
        mine = jnp.where(is_idle, idles, singles)
        return (
            idles + is_idle.astype(jnp.int32),
            singles + is_single.astype(jnp.int32),
            jnp.where(o == me, mine, rank),
        )

    zero = jnp.int32(0)
    job_ref[0] = side
    job_ref[1] = held_ref[me]
    job_ref[2] = lax.fori_loop(0, owners, fill, (zero, zero, zero), unroll=8)[2]
    copy.wait()


def make_plan(block_owner, gradient, owners):
    blocks, rows, width = gradient.shape
    sizes = (2 * owners, blocks, owners, owners, 3)
    *tables, mine = pl.pallas_call(
        plan_kernel,
        out_shape=[jax.ShapeDtypeStruct((n,), jnp.int32) for n in sizes]
        + [
            jax.ShapeDtypeStruct((blocks, rows, width // 2), jnp.float32),
        ],
        in_specs=[SMEM, ANY],
        out_specs=[SMEM] * len(sizes) + [WHOLE],
        scratch_shapes=[pltpu.SMEM((owners,), jnp.int32), pltpu.SemaphoreType.DMA],
        compiler_params=pltpu.CompilerParams(vmem_limit_bytes=4 * MIB),
        cost_estimate=pl.CostEstimate(flops=0, bytes_accessed=4 << 20, transcendentals=0),
        name="plan",
    )(in_hbm(block_owner), in_hbm(gradient))
    return tables + [mine]


def room_kernel(out_ref):
    pass


def make_room(shape):
    return pl.pallas_call(
        room_kernel,
        out_specs=ANY,
        out_shape=jax.ShapeDtypeStruct(shape, jnp.bfloat16),
        compiler_params=pltpu.CompilerParams(vmem_limit_bytes=60 * MIB),
        name="room",
    )()


def dispatch_kernel(job_ref, send_ref, mine_ref, other_ref, _, out_ref, ready, sems):
    dests, _, width = ready.shape
    half = width // 2
    here = pl.ds(pl.multiple_of(job_ref[0] * half, half), half)
    steps = sems.shape[0]
    count = dests // steps

    def one(dest, carry):
        for slot in range(2):
            b = send_ref[2 * dest + slot]
            ready[dest, :, slot * half : (slot + 1) * half] = (
                mine_ref[b] + other_ref[b, :, here]
            ).astype(jnp.bfloat16)
        return carry

    copies = []
    for step in range(steps):
        lax.fori_loop(step * count, (step + 1) * count, one, 0, unroll=4)
        part = pl.ds(step * count, count)
        copies.append(pltpu.make_async_copy(ready.at[part], out_ref.at[part], sems.at[step]))
        copies[-1].start()
    for copy in copies:
        copy.wait()


def dispatch(job, send, mine, other, room):
    shape = room.shape
    return pl.pallas_call(
        dispatch_kernel,
        in_specs=[SMEM, SMEM, WHOLE, WHOLE, ANY],
        out_specs=ANY,
        out_shape=jax.ShapeDtypeStruct(shape, jnp.bfloat16),
        input_output_aliases={4: 0},
        scratch_shapes=[pltpu.VMEM(shape, jnp.bfloat16), pltpu.SemaphoreType.DMA((4,))],
        compiler_params=pltpu.CompilerParams(vmem_limit_bytes=16 * MIB),
        cost_estimate=pl.CostEstimate(flops=0, bytes_accessed=5 << 20, transcendentals=0),
        name="dispatch",
    )(job, send, in_vmem(mine), other, in_hbm(room))


def product(a, b, dims):
    return lax.dot_general(
        a, b, ((dims[:1], dims[1:]), ((), ())), preferred_element_type=jnp.float32
    )


def begin_kernel(
    job_ref, own_ref, left_own, left_other, right_own, left_ref, right_ref, total_ref, sems
):
    _, width = own_ref.shape
    half = width // 2
    here = pl.multiple_of(job_ref[0] * half, half)
    there = pl.multiple_of(half - job_ref[0] * half, half)
    held = job_ref[1]
    rights = [
        pltpu.make_async_copy(right_own.at[slot], right_ref.at[slot], sems.at[slot])
        for slot in range(2)
    ]
    lefts = [
        pltpu.make_async_copy(source, left_ref.at[:, :, pl.ds(start, half)], sems.at[2 + i])
        for i, (source, start) in enumerate(((left_own, here), (left_other, there)))
    ]
    for copy in rights + lefts:
        copy.start()
    for slot in range(2):
        rights[slot].wait()

        @pl.when(held > slot)
        def _():
            span = pl.ds(slot * half, half)
            for at in range(0, own_ref.shape[0], TILE):
                rows = pl.ds(at, TILE)
                total_ref[slot, rows, :] = product(
                    own_ref[rows, span], right_ref[slot, pl.ds(here, half), :], (1, 0)
                )

    for copy in lefts:
        copy.wait()


def begin_updates(job, own, left_own, left_other, right_own):
    size = own.shape[0]
    half = size // 2
    bf16 = jnp.bfloat16
    begun = pl.pallas_call(
        begin_kernel,
        in_specs=[SMEM, WHOLE] + [ANY] * 3,
        out_specs=[WHOLE] * 3,
        out_shape=[
            jax.ShapeDtypeStruct((2, size, size), bf16),
            jax.ShapeDtypeStruct((2, size, half), bf16),
            jax.ShapeDtypeStruct((2, size, half), jnp.float32),
        ],
        scratch_shapes=[pltpu.SemaphoreType.DMA((4,))],
        compiler_params=pltpu.CompilerParams(vmem_limit_bytes=20 * MIB),
        cost_estimate=pl.CostEstimate(
            flops=4 * size * half * half, bytes_accessed=16 << 20, transcendentals=0
        ),
        name="begin",
    )(job, own, in_hbm(left_own), in_hbm(left_other), in_hbm(right_own))
    return [in_vmem(value) for value in begun]


def jobs_kernel(
    job_ref, own_ref, other_ref, left, right, total_ref, out_ref, applied
):
    size, width = own_ref.shape
    half = width // 2
    quarter = half // PIECES
    side = job_ref[0]
    held = job_ref[1]
    rank = job_ref[2]
    here = pl.multiple_of(side * half, half)
    there = pl.multiple_of(half - side * half, half)

    def tiles(count, body):
        for at in range(0, count, TILE):
            body(at)

    def rows_at(start):
        return pl.ds(pl.multiple_of(start, TILE), TILE)

    def right_half(slot):
        span = pl.ds(slot * half, half)

        def body(at):
            rows = rows_at(at)
            total = product(other_ref[rows, span], right[slot, pl.ds(there, half), :], (1, 0))
            applied[slot, rows, :] = (total + total_ref[slot, rows, :]).astype(jnp.bfloat16)

        tiles(size, body)

    def left_half(slot):
        span = pl.ds(slot * half, half)

        def body(at):
            rows = rows_at(at)
            out_ref[rows, span] = product(left[slot, rows, :], applied[slot], (1, 0)).astype(
                jnp.bfloat16
            )

        tiles(size, body)

    def left_gram(slot, start, count, target):
        span = pl.ds(slot * half, half)
        wanted = pl.ds(pl.multiple_of(here + start, quarter), count)

        def body(at):
            rows = rows_at(at)
            total = product(own_ref[rows, span], own_ref[wanted, span], (1, 1))
            total += product(other_ref[rows, span], other_ref[wanted, span], (1, 1))
            out_ref[rows, target] = total.astype(jnp.bfloat16)

        tiles(size, body)

    def right_gram(slot, start, count, target):
        wanted = pl.ds(pl.multiple_of(slot * half + start, quarter), count)
        for source, offset in ((own_ref, here), (other_ref, there)):

            def body(at):
                span = pl.ds(pl.multiple_of(slot * half + at, TILE), TILE)
                total = product(source[:, span], own_ref[:, wanted], (0, 0))
                out_ref[rows_at(offset + at), target] = total.astype(jnp.bfloat16)

            tiles(half, body)

    first_part = pl.ds(0, half)
    second_part = pl.ds(half, half)
    last_part = pl.ds(width, quarter)

    @pl.when(held == 2)
    def _():
        right_half(0)
        right_half(1)
        left_half(0)
        left_half(1)

    @pl.when(held == 1)
    def _():
        right_half(0)

    @pl.when(held == 0)
    def _():
        left_gram(0, 0, half, first_part)
        right_gram(0, 0, half, second_part)

    @pl.when((held == 1) & (rank % 2 == 0))
    def _():
        left_gram(1, 0, half, second_part)
        left_half(0)

    @pl.when((held == 1) & (rank % 2 == 1))
    def _():
        right_gram(1, 0, half, second_part)
        left_half(0)

    piece = rank % (2 * PIECES)
    start = (piece % PIECES) * quarter

    @pl.when((held == 0) & (piece < PIECES))
    def _():
        left_gram(1, start, quarter, last_part)

    @pl.when((held == 0) & (piece >= PIECES))
    def _():
        right_gram(1, start, quarter, last_part)


def run_jobs(job, own, other, left, right, total):
    size = own.shape[0]
    half = size // 2
    width = size + half // PIECES
    bf16 = jnp.bfloat16
    return pl.pallas_call(
        jobs_kernel,
        in_specs=[SMEM] + [WHOLE] * 5,
        out_specs=WHOLE,
        out_shape=jax.ShapeDtypeStruct((size, width), bf16),
        scratch_shapes=[pltpu.VMEM((2, size, half), bf16)],
        compiler_params=pltpu.CompilerParams(vmem_limit_bytes=20 * MIB),
        cost_estimate=pl.CostEstimate(
            flops=8 * size * size * half, bytes_accessed=12 << 20, transcendentals=0
        ),
        name="jobs",
    )(job, own, other, left, right, total)


def finish_kernel(
    spot_ref,
    idle_ref,
    single_ref,
    back_ref,
    left_ref,
    right_ref,
    left_out,
    right_out,
    update_out,
    new_left,
    new_right,
    update,
    sems,
):
    blocks, _, half = left_ref.shape
    owners = back_ref.shape[0]
    quarter = half // PIECES
    idle_blocks, split_from = whole_gram_counts(blocks, owners)
    f32 = jnp.float32

    def part(source, slot):
        return back_ref[source, :, slot * half : (slot + 1) * half].astype(f32)

    def applied(b):
        spot = spot_ref[b]
        column = pl.multiple_of((spot % 2) * half, half)
        update[b] = back_ref[spot // 2, :, pl.ds(column, half)]

    def whole_pair(b, carry):
        applied(b)
        source = idle_ref[b]
        new_left[b] = left_ref[b] + part(source, 0)
        new_right[b] = right_ref[b] + part(source, 1)
        return carry

    def shared_pair(b, carry):
        applied(b)
        at = 2 * (b - idle_blocks)
        new_left[b] = left_ref[b] + part(single_ref[at], 1)
        new_right[b] = right_ref[b] + part(single_ref[at + 1], 1)
        return carry

    def split_pair(b, carry):
        applied(b)
        at = 2 * PIECES * (b - split_from)
        last = pl.ds(2 * half, quarter)
        for k in range(PIECES):
            span = pl.ds(k * quarter, quarter)
            for new, old, source in (
                (new_left, left_ref, idle_ref[at + k]),
                (new_right, right_ref, idle_ref[at + PIECES + k]),
            ):
                new[b, :, span] = old[b, :, span] + back_ref[source, :, last].astype(f32)
        return carry

    copies = []

    def send(first, last):
        span = pl.ds(first, last - first)
        for source, target in ((new_left, left_out), (new_right, right_out), (update, update_out)):
            copy = pltpu.make_async_copy(source.at[span], target.at[span], sems.at[len(copies)])
            copy.start()
            copies.append(copy)

    third = idle_blocks // 3
    for first in range(0, idle_blocks, third):
        lax.fori_loop(first, first + third, whole_pair, 0, unroll=2)
        send(first, first + third)
    lax.fori_loop(idle_blocks, split_from, shared_pair, 0, unroll=2)
    lax.fori_loop(split_from, blocks, split_pair, 0)
    send(idle_blocks, blocks)
    for copy in copies:
        copy.wait()


def finish(spot, idle, single, back, left_stats, right_stats):
    shape = left_stats.shape
    kinds = (jnp.float32, jnp.float32, jnp.bfloat16)
    return pl.pallas_call(
        finish_kernel,
        in_specs=[SMEM] * 3 + [WHOLE] * 3,
        out_specs=[ANY] * 3,
        out_shape=[jax.ShapeDtypeStruct(shape, kind) for kind in kinds],
        scratch_shapes=[pltpu.VMEM(shape, kind) for kind in kinds]
        + [pltpu.SemaphoreType.DMA((12,))],
        compiler_params=pltpu.CompilerParams(vmem_limit_bytes=16 * MIB),
        cost_estimate=pl.CostEstimate(flops=0, bytes_accessed=9 << 20, transcendentals=0),
        name="finish",
    )(spot, idle, single, back, left_stats, right_stats)


def per_device(gradients, left_stats, right_stats, left_root, right_root, block_owner):
    owners = lax.axis_size("shard")
    blocks, rows, half = left_stats.shape
    size = 2 * half
    swapped = partial(lax.ppermute, axis_name="rep", perm=[(0, 1), (1, 0)])
    gradient = gradients[0]
    other_gradient = swapped(gradient)
    send, spot, idle, single, job, mine = make_plan(block_owner, gradient, owners)
    room = make_room((owners, rows, size))
    outgoing = dispatch(job, send, mine, other_gradient, room)
    other_left = swapped(left_root[0])
    arrived = lax.all_to_all(outgoing, "shard", split_axis=0, concat_axis=0, tiled=True)
    own = arrived.reshape(size, size)
    other = swapped(own)
    begun = begin_updates(job, own, left_root[0], other_left, right_root[0])
    results = run_jobs(job, own, other, *begun)
    back = lax.all_to_all(
        results.reshape(owners, rows, -1), "shard", split_axis=0, concat_axis=0, tiled=True
    )
    return tuple(finish(spot, idle, single, back, left_stats, right_stats))


def solution(mesh):
    return jax.shard_map(
        per_device,
        mesh=mesh,
        in_specs=(
            P("rep", None, "shard", None),
            P(None, "shard", "rep"),
            P(None, "shard", "rep"),
            P("shard", None, None, "rep"),
            P("shard", None, None, "rep"),
            P(),
        ),
        out_specs=(P(None, "shard", "rep"), P(None, "shard", "rep"), P(None, "shard", "rep")),
        check_vma=False,
    )
```

```python
from functools import partial

import jax
import jax.numpy as jnp
from jax import lax
from jax.experimental import pallas as pl
from jax.experimental.pallas import tpu as pltpu
from jax.sharding import PartitionSpec as P

DOUBLE = 32
SINGLE = 24
PIECES = 4
SMEM = pl.BlockSpec(memory_space=pltpu.SMEM)
WHOLE = pl.BlockSpec(memory_space=pltpu.VMEM)
ANY = pl.BlockSpec(memory_space=pl.ANY)
MIB = 1024 * 1024
TILE = 1024


def in_hbm(value):
    return pltpu.with_memory_space_constraint(value, pltpu.HBM)


def in_vmem(value):
    return pltpu.with_memory_space_constraint(value, pltpu.VMEM)


def whole_gram_counts(blocks, owners):
    idle = owners - DOUBLE - SINGLE
    shared = SINGLE // 2
    return idle, idle + shared


def plan_kernel(
    owner_ref,
    gradient_ref,
    send_ref,
    spot_ref,
    idle_ref,
    single_ref,
    job_ref,
    mine_ref,
    held_ref,
    sem,
):
    blocks = owner_ref.shape[0]
    owners = held_ref.shape[0]
    half = mine_ref.shape[-1]
    side = lax.axis_index("rep")
    me = lax.axis_index("shard")
    here = pl.ds(pl.multiple_of(side * half, half), half)
    copy = pltpu.make_async_copy(gradient_ref.at[:, :, here], mine_ref, sem)
    copy.start()
    idle_blocks, split_from = whole_gram_counts(blocks, owners)
    pieces = 2 * PIECES * (blocks - split_from)

    def clear(o, carry):
        held_ref[o] = 0
        return carry

    lax.fori_loop(0, owners, clear, 0, unroll=8)

    def place(b, carry):
        o = owner_ref[b]
        slot = held_ref[o]
        send_ref[2 * o + slot] = b
        spot_ref[b] = 2 * o + slot
        held_ref[o] = slot + 1
        return carry

    lax.fori_loop(0, blocks, place, 0, unroll=8)

    def fill(o, carry):
        idles, singles, rank = carry
        held = held_ref[o]
        is_idle = held == 0
        is_single = held == 1
        idle_ref[jnp.where(is_idle, idles, owners - 1)] = o
        single_ref[jnp.where(is_single, singles, owners - 1)] = o
        extra = jnp.where(idles < pieces, split_from + idles // (2 * PIECES), 0)
        send_ref[2 * o] = jnp.where(is_idle, idles, send_ref[2 * o])
        send_ref[2 * o + 1] = jnp.where(
            is_idle,
            extra,
            jnp.where(is_single, idle_blocks + singles // 2, send_ref[2 * o + 1]),
        )
        mine = jnp.where(is_idle, idles, singles)
        return (
            idles + is_idle.astype(jnp.int32),
            singles + is_single.astype(jnp.int32),
            jnp.where(o == me, mine, rank),
        )

    zero = jnp.int32(0)
    job_ref[0] = side
    job_ref[1] = held_ref[me]
    job_ref[2] = lax.fori_loop(0, owners, fill, (zero, zero, zero), unroll=8)[2]
    copy.wait()


def make_plan(block_owner, gradient, owners):
    blocks, rows, width = gradient.shape
    sizes = (2 * owners, blocks, owners, owners, 3)
    *tables, mine = pl.pallas_call(
        plan_kernel,
        out_shape=[jax.ShapeDtypeStruct((n,), jnp.int32) for n in sizes]
        + [
            jax.ShapeDtypeStruct((blocks, rows, width // 2), jnp.float32),
        ],
        in_specs=[SMEM, ANY],
        out_specs=[SMEM] * len(sizes) + [WHOLE],
        scratch_shapes=[pltpu.SMEM((owners,), jnp.int32), pltpu.SemaphoreType.DMA],
        compiler_params=pltpu.CompilerParams(vmem_limit_bytes=4 * MIB),
        cost_estimate=pl.CostEstimate(flops=0, bytes_accessed=4 << 20, transcendentals=0),
        name="plan",
    )(in_hbm(block_owner), in_hbm(gradient))
    return tables + [mine]


def room_kernel(out_ref):
    pass


def make_room(shape):
    return pl.pallas_call(
        room_kernel,
        out_specs=ANY,
        out_shape=jax.ShapeDtypeStruct(shape, jnp.bfloat16),
        compiler_params=pltpu.CompilerParams(vmem_limit_bytes=60 * MIB),
        name="room",
    )()


def dispatch_kernel(job_ref, send_ref, mine_ref, other_ref, _, out_ref, ready, sems):
    dests, _, width = ready.shape
    half = width // 2
    here = pl.ds(pl.multiple_of(job_ref[0] * half, half), half)
    steps = sems.shape[0]
    count = dests // steps

    def one(dest, carry):
        for slot in range(2):
            b = send_ref[2 * dest + slot]
            ready[dest, :, slot * half : (slot + 1) * half] = (
                mine_ref[b] + other_ref[b, :, here]
            ).astype(jnp.bfloat16)
        return carry

    copies = []
    for step in range(steps):
        lax.fori_loop(step * count, (step + 1) * count, one, 0, unroll=4)
        part = pl.ds(step * count, count)
        copies.append(pltpu.make_async_copy(ready.at[part], out_ref.at[part], sems.at[step]))
        copies[-1].start()
    for copy in copies:
        copy.wait()


def dispatch(job, send, mine, other, room):
    shape = room.shape
    return pl.pallas_call(
        dispatch_kernel,
        in_specs=[SMEM, SMEM, WHOLE, WHOLE, ANY],
        out_specs=ANY,
        out_shape=jax.ShapeDtypeStruct(shape, jnp.bfloat16),
        input_output_aliases={4: 0},
        scratch_shapes=[pltpu.VMEM(shape, jnp.bfloat16), pltpu.SemaphoreType.DMA((4,))],
        compiler_params=pltpu.CompilerParams(vmem_limit_bytes=16 * MIB),
        cost_estimate=pl.CostEstimate(flops=0, bytes_accessed=5 << 20, transcendentals=0),
        name="dispatch",
    )(job, send, in_vmem(mine), other, in_hbm(room))


def product(a, b, dims):
    return lax.dot_general(
        a, b, ((dims[:1], dims[1:]), ((), ())), preferred_element_type=jnp.float32
    )


def begin_kernel(
    job_ref, own_ref, left_own, left_other, right_own, left_ref, right_ref, total_ref, sems
):
    _, width = own_ref.shape
    half = width // 2
    here = pl.multiple_of(job_ref[0] * half, half)
    there = pl.multiple_of(half - job_ref[0] * half, half)
    held = job_ref[1]
    rights = [
        pltpu.make_async_copy(right_own.at[slot], right_ref.at[slot], sems.at[slot])
        for slot in range(2)
    ]
    lefts = [
        pltpu.make_async_copy(source, left_ref.at[:, :, pl.ds(start, half)], sems.at[2 + i])
        for i, (source, start) in enumerate(((left_own, here), (left_other, there)))
    ]
    for copy in rights + lefts:
        copy.start()
    for slot in range(2):
        rights[slot].wait()

        @pl.when(held > slot)
        def _():
            span = pl.ds(slot * half, half)
            for at in range(0, own_ref.shape[0], TILE):
                rows = pl.ds(at, TILE)
                total_ref[slot, rows, :] = product(
                    own_ref[rows, span], right_ref[slot, pl.ds(here, half), :], (1, 0)
                )

    for copy in lefts:
        copy.wait()


def begin_updates(job, own, left_own, left_other, right_own):
    size = own.shape[0]
    half = size // 2
    bf16 = jnp.bfloat16
    begun = pl.pallas_call(
        begin_kernel,
        in_specs=[SMEM, WHOLE] + [ANY] * 3,
        out_specs=[WHOLE] * 3,
        out_shape=[
            jax.ShapeDtypeStruct((2, size, size), bf16),
            jax.ShapeDtypeStruct((2, size, half), bf16),
            jax.ShapeDtypeStruct((2, size, half), jnp.float32),
        ],
        scratch_shapes=[pltpu.SemaphoreType.DMA((4,))],
        compiler_params=pltpu.CompilerParams(vmem_limit_bytes=20 * MIB),
        cost_estimate=pl.CostEstimate(
            flops=4 * size * half * half, bytes_accessed=16 << 20, transcendentals=0
        ),
        name="begin",
    )(job, own, in_hbm(left_own), in_hbm(left_other), in_hbm(right_own))
    return [in_vmem(value) for value in begun]


def jobs_kernel(
    job_ref, own_ref, other_ref, left, right, total_ref, out_ref, applied
):
    size, width = own_ref.shape
    half = width // 2
    quarter = half // PIECES
    side = job_ref[0]
    held = job_ref[1]
    rank = job_ref[2]
    here = pl.multiple_of(side * half, half)
    there = pl.multiple_of(half - side * half, half)

    def tiles(count, body):
        for at in range(0, count, TILE):
            body(at)

    def rows_at(start):
        return pl.ds(pl.multiple_of(start, TILE), TILE)

    def right_half(slot):
        span = pl.ds(slot * half, half)

        def body(at):
            rows = rows_at(at)
            total = product(other_ref[rows, span], right[slot, pl.ds(there, half), :], (1, 0))
            applied[slot, rows, :] = (total + total_ref[slot, rows, :]).astype(jnp.bfloat16)

        tiles(size, body)

    def left_half(slot):
        span = pl.ds(slot * half, half)

        def body(at):
            rows = rows_at(at)
            out_ref[rows, span] = product(left[slot, rows, :], applied[slot], (1, 0)).astype(
                jnp.bfloat16
            )

        tiles(size, body)

    def left_gram(slot, start, count, target):
        span = pl.ds(slot * half, half)
        wanted = pl.ds(pl.multiple_of(here + start, quarter), count)

        def body(at):
            rows = rows_at(at)
            total = product(own_ref[rows, span], own_ref[wanted, span], (1, 1))
            total += product(other_ref[rows, span], other_ref[wanted, span], (1, 1))
            out_ref[rows, target] = total.astype(jnp.bfloat16)

        tiles(size, body)

    def right_gram(slot, start, count, target):
        wanted = pl.ds(pl.multiple_of(slot * half + start, quarter), count)
        for source, offset in ((own_ref, here), (other_ref, there)):

            def body():
                span = pl.ds(pl.multiple_of(slot * half, half), half)
                total = product(source[:, span], own_ref[:, wanted], (0, 0))
                out_ref[pl.ds(offset, half), target] = total.astype(jnp.bfloat16)

            body()

    first_part = pl.ds(0, half)
    second_part = pl.ds(half, half)
    last_part = pl.ds(width, quarter)

    @pl.when(held == 2)
    def _():
        right_half(0)
        right_half(1)
        left_half(0)
        left_half(1)

    @pl.when(held == 1)
    def _():
        right_half(0)

    @pl.when(held == 0)
    def _():
        left_gram(0, 0, half, first_part)
        right_gram(0, 0, half, second_part)

    @pl.when((held == 1) & (rank % 2 == 0))
    def _():
        left_gram(1, 0, half, second_part)
        left_half(0)

    @pl.when((held == 1) & (rank % 2 == 1))
    def _():
        right_gram(1, 0, half, second_part)
        left_half(0)

    piece = rank % (2 * PIECES)
    start = (piece % PIECES) * quarter

    @pl.when((held == 0) & (piece < PIECES))
    def _():
        left_gram(1, start, quarter, last_part)

    @pl.when((held == 0) & (piece >= PIECES))
    def _():
        right_gram(1, start, quarter, last_part)


def run_jobs(job, own, other, left, right, total):
    size = own.shape[0]
    half = size // 2
    width = size + half // PIECES
    bf16 = jnp.bfloat16
    return pl.pallas_call(
        jobs_kernel,
        in_specs=[SMEM] + [WHOLE] * 5,
        out_specs=WHOLE,
        out_shape=jax.ShapeDtypeStruct((size, width), bf16),
        scratch_shapes=[pltpu.VMEM((2, size, half), bf16)],
        compiler_params=pltpu.CompilerParams(vmem_limit_bytes=20 * MIB),
        cost_estimate=pl.CostEstimate(
            flops=8 * size * size * half, bytes_accessed=12 << 20, transcendentals=0
        ),
        name="jobs",
    )(job, own, other, left, right, total)


def finish_kernel(
    spot_ref,
    idle_ref,
    single_ref,
    back_ref,
    left_ref,
    right_ref,
    left_out,
    right_out,
    update_out,
    new_left,
    new_right,
    update,
    sems,
):
    blocks, _, half = left_ref.shape
    owners = back_ref.shape[0]
    quarter = half // PIECES
    idle_blocks, split_from = whole_gram_counts(blocks, owners)
    f32 = jnp.float32

    def part(source, slot):
        return back_ref[source, :, slot * half : (slot + 1) * half].astype(f32)

    def applied(b):
        spot = spot_ref[b]
        column = pl.multiple_of((spot % 2) * half, half)
        update[b] = back_ref[spot // 2, :, pl.ds(column, half)]

    def whole_pair(b, carry):
        applied(b)
        source = idle_ref[b]
        new_left[b] = left_ref[b] + part(source, 0)
        new_right[b] = right_ref[b] + part(source, 1)
        return carry

    def shared_pair(b, carry):
        applied(b)
        at = 2 * (b - idle_blocks)
        new_left[b] = left_ref[b] + part(single_ref[at], 1)
        new_right[b] = right_ref[b] + part(single_ref[at + 1], 1)
        return carry

    def split_pair(b, carry):
        applied(b)
        at = 2 * PIECES * (b - split_from)
        last = pl.ds(2 * half, quarter)
        for k in range(PIECES):
            span = pl.ds(k * quarter, quarter)
            for new, old, source in (
                (new_left, left_ref, idle_ref[at + k]),
                (new_right, right_ref, idle_ref[at + PIECES + k]),
            ):
                new[b, :, span] = old[b, :, span] + back_ref[source, :, last].astype(f32)
        return carry

    copies = []

    def send(first, last):
        span = pl.ds(first, last - first)
        for source, target in ((new_left, left_out), (new_right, right_out), (update, update_out)):
            copy = pltpu.make_async_copy(source.at[span], target.at[span], sems.at[len(copies)])
            copy.start()
            copies.append(copy)

    step = idle_blocks // 4
    for first in range(0, idle_blocks, step):
        lax.fori_loop(first, first + step, whole_pair, 0, unroll=2)
        send(first, first + step)
    lax.fori_loop(idle_blocks, split_from, shared_pair, 0, unroll=2)
    lax.fori_loop(split_from, blocks, split_pair, 0)
    send(idle_blocks, blocks)
    for copy in copies:
        copy.wait()


def finish(spot, idle, single, back, left_stats, right_stats):
    shape = left_stats.shape
    kinds = (jnp.float32, jnp.float32, jnp.bfloat16)
    return pl.pallas_call(
        finish_kernel,
        in_specs=[SMEM] * 3 + [WHOLE] * 3,
        out_specs=[ANY] * 3,
        out_shape=[jax.ShapeDtypeStruct(shape, kind) for kind in kinds],
        scratch_shapes=[pltpu.VMEM(shape, kind) for kind in kinds]
        + [pltpu.SemaphoreType.DMA((15,))],
        compiler_params=pltpu.CompilerParams(vmem_limit_bytes=16 * MIB),
        cost_estimate=pl.CostEstimate(flops=0, bytes_accessed=9 << 20, transcendentals=0),
        name="finish",
    )(spot, idle, single, back, left_stats, right_stats)


def per_device(gradients, left_stats, right_stats, left_root, right_root, block_owner):
    owners = lax.axis_size("shard")
    blocks, rows, half = left_stats.shape
    size = 2 * half
    swapped = partial(lax.ppermute, axis_name="rep", perm=[(0, 1), (1, 0)])
    gradient = gradients[0]
    other_gradient = swapped(gradient)
    send, spot, idle, single, job, mine = make_plan(block_owner, gradient, owners)
    room = make_room((owners, rows, size))
    outgoing = dispatch(job, send, mine, other_gradient, room)
    other_left = swapped(left_root[0])
    arrived = lax.all_to_all(outgoing, "shard", split_axis=0, concat_axis=0, tiled=True)
    own = arrived.reshape(size, size)
    other = swapped(own)
    begun = begin_updates(job, own, left_root[0], other_left, right_root[0])
    results = run_jobs(job, own, other, *begun)
    back = lax.all_to_all(
        results.reshape(owners, rows, -1), "shard", split_axis=0, concat_axis=0, tiled=True
    )
    return tuple(finish(spot, idle, single, back, left_stats, right_stats))


def solution(mesh):
    return jax.shard_map(
        per_device,
        mesh=mesh,
        in_specs=(
            P("rep", None, "shard", None),
            P(None, "shard", "rep"),
            P(None, "shard", "rep"),
            P("shard", None, None, "rep"),
            P("shard", None, None, "rep"),
            P(),
        ),
        out_specs=(P(None, "shard", "rep"), P(None, "shard", "rep"), P(None, "shard", "rep")),
        check_vma=False,
    )
```
